512 devices in a mesh: dp: 32 (over y, x, core), tensor: 16 (over z).
Axes of the slice: x: 4, y: 4, z: 16, core: 2. Of those that a mesh axis runs over, the one named last changes fastest.
Arguments:
- attn_out: bfloat16 [3, 2048, 4096], P(None, 'dp', 'tensor'), may hold values from -6 to 6
- base_weight: bfloat16 [4096, 4096], P('tensor'), may hold values from -0.09375 to 0.09375
- store_a: bfloat16 [128, 4096, 128], P('dp', 'tensor'), may hold values from -0.09375 to 0.09375
- store_b: bfloat16 [128, 128, 4096], P('dp', None, 'tensor'), may hold values from -0.5 to 0.5
- adapter_lists: int32 [32, 16], P('dp'), may hold values from 0 to 127, as said below
- placement_map: int32 [128], replicated, may hold values from 0 to 127, as said below
- request_slot: int32 [2048], P('dp'), may hold values from 0 to 15
Outputs:
- projected: bfloat16 [3, 2048, 4096], P(None, 'dp', 'tensor')
The draws below stay inside these ranges and needn't reach their ends.
Inputs may be any that keep to these rules, and one draw needn't show every extreme that they name: `adapter_lists`: each replica's 16 adapters are stored on 16 different indices of dp. `placement_map` is a permutation; adapter a's panels are row placement_map[a] of the stores, held by index placement_map[a] // 4 of dp.
All inputs are finite; a program needn't handle non-finite values.
Results may differ from the reference program's by a relative error of at most 0.001.
Values may be sent and summed in bfloat16 or wider, within the bound.
No kernel may reach another device: no remote copies, remote signals or barrier semaphores. Data moves between devices by JAX's collectives and lax.ppermute only.
A program may use at most 64 MiB of HBM per device.

```python
import math
import jax
import jax.numpy as jnp
import numpy as np
from jax import lax

OUTPUT_FEATURES = 4096
RANK = 128
DECODE_STEPS = 3
REQ_DEV = 64
STORE_DEV = 4
REPLICAS = 32
SLOTS = 16
ADAPTERS = 128
TOTAL_REQUESTS = 2048
IN = 4096


def lookup_tables(key):
    position_of = jax.random.permutation(jax.random.fold_in(key, 101), ADAPTERS).astype(jnp.int32)
    holder = jnp.argsort(position_of, stable=True).astype(jnp.int32)

    def one_list(list_key):
        device_key, slot_key = jax.random.split(list_key)
        chosen = jax.random.permutation(device_key, REPLICAS)[:SLOTS].astype(jnp.int32)
        local_slot = jax.random.randint(slot_key, (SLOTS,), 0, STORE_DEV, dtype=jnp.int32)
        return holder[chosen * STORE_DEV + local_slot]
    replica_lists = jax.vmap(one_list)(jax.random.split(jax.random.fold_in(key, 202), REPLICAS))
    return (position_of, replica_lists.astype(jnp.int32))


def draw_placement_map(key, part):
    return lookup_tables(key)[0]


def draw_adapter_lists(key, part):
    return lookup_tables(key)[1]


def set_ends(entries, stream_key, smallest, largest):
    spot = [jax.random.randint(jax.random.fold_in(stream_key, axis), (), 0, length) for axis, length in enumerate(entries.shape)]
    main_axis = entries.shape.index(max(entries.shape))
    next_to = spot[:main_axis] + [(spot[main_axis] + 1) % entries.shape[main_axis]] + spot[main_axis + 1:]
    return entries.at[tuple(spot)].set(smallest).at[tuple(next_to)].set(largest)


def levels(key, dims, pieces, low, top_value):
    factor_of, own = 1.0, jax.random.fold_in(key, 6)
    for dim, blocks in pieces:
        draws = jnp.exp(jax.random.uniform(jax.random.fold_in(own, dim), (blocks,), jnp.float32, low / len(pieces), top_value / len(pieces)))
        factor_of = factor_of * jnp.repeat(draws, dims[dim] // blocks).reshape([-1 if axis == dim else 1 for axis in range(len(dims))])
    return factor_of


def rank_table(amount, lean):
    loads = [(1 << 20) // math.isqrt(standing ** lean) + 1 for standing in range(1, amount + 1)]
    scale = 1 + sum(loads) // (1 << 30)
    return np.cumsum(np.array([max(1, weight // scale) for weight in loads]))


def ranked(own_key, shape, count, skew):
    grid = rank_table(count, skew)
    ticket = jax.random.randint(jax.random.fold_in(own_key, 1), shape, 0, int(grid[count - 1]))
    grade = jnp.searchsorted(jnp.asarray(grid, jnp.int32), ticket, side="right")
    return jax.random.permutation(jax.random.fold_in(own_key, 2), count)[grade].astype(jnp.int32)


def normal_values(rng, extent, width, limit, cuts=(), held_as=jnp.bfloat16):
    loudness = levels(rng, extent, cuts, -0.22, 0.18) if cuts else 1.0
    result = jax.random.normal(rng, extent, jnp.float32) * width * loudness
    return jnp.minimum(jnp.maximum(result, -limit), limit).astype(held_as)


def setup_inputs(seed: int = 0) -> dict:
    arg_keys = jax.random.split(jax.random.key(seed), 8)
    return {
        "attn_out": normal_values(arg_keys[0], (DECODE_STEPS, TOTAL_REQUESTS, IN), 1.0, 6.0, ((1, 32), (2, 16))),
        "base_weight": normal_values(arg_keys[1], (IN, OUTPUT_FEATURES), IN ** -0.5, 0.09375, ((0, 16),)),
        "store_a": normal_values(arg_keys[2], (ADAPTERS, IN, RANK), IN ** -0.5, 0.09375, ((0, 32), (1, 16))),
        "store_b": normal_values(arg_keys[3], (ADAPTERS, RANK, OUTPUT_FEATURES), RANK ** -0.5, 0.5, ((0, 32), (2, 16))),
        "adapter_lists": draw_adapter_lists(jax.random.fold_in(arg_keys[7], 71), 0),
        "placement_map": draw_placement_map(jax.random.fold_in(arg_keys[7], 71), 0),
        "request_slot": set_ends(ranked(arg_keys[6], (TOTAL_REQUESTS,), SLOTS, 2), jax.random.fold_in(arg_keys[6], 3), 0, SLOTS - 1).astype(jnp.int32),
    }


def reference(attn_out, base_weight, store_a, store_b, adapter_lists, placement_map, request_slot):
    flat_rows = attn_out.reshape(DECODE_STEPS * TOTAL_REQUESTS, IN)
    base_output_sum = jnp.dot(flat_rows, base_weight, preferred_element_type=jnp.float32)
    replica = jnp.arange(TOTAL_REQUESTS, dtype=jnp.int32) // REQ_DEV
    adapter = adapter_lists[replica, request_slot]
    position = placement_map[adapter]
    grouped_input = attn_out.reshape(DECODE_STEPS, REPLICAS, REQ_DEV, IN).transpose(1, 0, 2, 3)
    grouped_positions = position.reshape(REPLICAS, REQ_DEV)

    def low_rank_group(step_operands):
        request_inputs, where_at = step_operands
        down_panel = store_a[where_at].astype(jnp.float32)
        up_panel = store_b[where_at].astype(jnp.float32)
        rank_reduce = jnp.einsum("maw,awv->mav", request_inputs.astype(jnp.float32), down_panel,
                            precision=lax.Precision.HIGHEST)
        return jnp.einsum("yja,jaz->yjz", rank_reduce, up_panel, precision=lax.Precision.HIGHEST)

    adapter_deltas = lax.map(low_rank_group, (grouped_input, grouped_positions))
    low_rank_delta = adapter_deltas.transpose(1, 0, 2, 3).reshape(DECODE_STEPS * TOTAL_REQUESTS, OUTPUT_FEATURES)
    return (base_output_sum + low_rank_delta).reshape(DECODE_STEPS, TOTAL_REQUESTS, OUTPUT_FEATURES).astype(jnp.bfloat16)
```

```python
import jax
import jax.numpy as jnp
from jax import lax
from jax.experimental import pallas as pl
from jax.experimental.pallas import tpu as pltpu
from jax.sharding import PartitionSpec as P

VMEM_BYTES = 24 * 1024 * 1024
WINDOW = 4


def local_call(body, outs, flops, moved, scalars, *arrays, scratch=()):
    smem = pl.BlockSpec(memory_space=pltpu.SMEM)
    vmem = pl.BlockSpec(memory_space=pltpu.VMEM)
    return pl.pallas_call(
        body,
        out_shape=outs,
        in_specs=[smem] * len(scalars) + [vmem] * len(arrays),
        out_specs=jax.tree.map(lambda _: vmem, outs),
        scratch_shapes=list(scratch),
        compiler_params=pltpu.CompilerParams(vmem_limit_bytes=VMEM_BYTES),
        cost_estimate=pl.CostEstimate(flops=flops, bytes_accessed=moved, transcendentals=0),
    )(*scalars, *arrays)


def wish_kernel(stored, list_ref, place_ref, wish_ref):
    wish_ref[...] = jnp.zeros_like(wish_ref)
    for s in range(list_ref.shape[1]):
        position = place_ref[list_ref[0, s]]
        slot = lax.rem(position, stored)
        wish_ref[lax.div(position, stored)] = jnp.full(wish_ref.shape[1:], slot, jnp.int32)


def hold_kernel(stored, steps, list_ref, place_ref, slot_ref, hold_ref):
    requests = slot_ref.shape[0]

    @pl.loop(0, requests, unroll=8)
    def _(r):
        holder = lax.div(place_ref[list_ref[0, slot_ref[r]]], stored)
        for step in range(steps):
            hold_ref[pl.ds(step * requests + r, 1), :] = jnp.full((1, 128), holder, jnp.int32)


def pick_kernel(asked_ref, store_ref, out_ref):
    @pl.loop(0, out_ref.shape[0])
    def _(q):
        out_ref[q] = store_ref[jnp.max(asked_ref[q])]


def turned(me_ref, ref):
    share = ref.shape[0] // WINDOW
    return [
        ref[pl.ds(pl.multiple_of(lax.rem(me_ref[0] + j, WINDOW) * share, share), share), :]
        for j in range(WINDOW)
    ]


def shrink_kernel(me_ref, hold_ref, x_ref, panels_ref, *refs):
    outs, total_ref = refs[:-1], refs[-1]
    hold = jnp.concatenate(turned(me_ref, hold_ref), axis=0)
    x = jnp.concatenate(turned(me_ref, x_ref), axis=0)
    total_ref[...] = jnp.zeros_like(total_ref)

    @pl.loop(0, panels_ref.shape[0], unroll=4)
    def _(q):
        product = jnp.dot(x, panels_ref[q], preferred_element_type=jnp.float32)
        total_ref[...] = jnp.where(hold == q, product, total_ref[...])

    share = total_ref.shape[0] // WINDOW
    for j, out_ref in enumerate(outs):
        out_ref[...] = total_ref[j * share:(j + 1) * share, :]


def final_kernel(me_ref, hold_ref, *refs):
    blocks, (panels_ref, base_ref, out_ref, total_ref) = refs[:WINDOW], refs[WINDOW:]
    hold = jnp.concatenate(turned(me_ref, hold_ref), axis=0)
    hold = jnp.concatenate([hold] * (total_ref.shape[1] // hold.shape[1]), axis=1)
    shrink = jnp.concatenate([b[...] for b in blocks], axis=0)
    high = shrink.astype(jnp.bfloat16)
    low = (shrink - high.astype(jnp.float32)).astype(jnp.bfloat16)
    both = jnp.concatenate([high, low], axis=1)
    total_ref[...] = jnp.zeros_like(total_ref)

    @pl.loop(0, panels_ref.shape[0], unroll=4)
    def _(q):
        panel = panels_ref[q]
        product = jnp.dot(
            both, jnp.concatenate([panel, panel], axis=0), preferred_element_type=jnp.float32
        )
        total_ref[...] = jnp.where(hold == q, product, total_ref[...])

    share = total_ref.shape[0] // WINDOW
    for j in range(WINDOW):
        begin = pl.multiple_of(lax.rem(me_ref[0] + j, WINDOW) * share, share)
        delta = total_ref[j * share:(j + 1) * share, :]
        here = base_ref[pl.ds(begin, share), :] + delta
        out_ref[pl.ds(begin, share), :] = here.astype(out_ref.dtype)


def shift(value, by, size):
    return lax.ppermute(value, "tensor", [(i, (i + by) % size) for i in range(size)])


def sum_over_tensor(parts):
    size = lax.axis_size("tensor")
    near = [shift(parts[1], 1, size), shift(parts[3], -1, size), shift(parts[2], -2, size)]
    mine = (parts[0] + near[0]) + (near[1] + near[2])
    far = [shift(mine, by, size) for by in (8, 4, -4)]
    mine = (mine + far[0]) + (far[1] + far[2])
    return [mine, shift(mine, -1, size), shift(mine, 2, size), shift(mine, 1, size)]


def on_device(attn_out, base_weight, store_a, store_b, adapter_lists, placement_map, request_slot):
    replicas = lax.axis_size("dp")
    columns = lax.axis_size("tensor")
    stored, depth, rank = store_a.shape
    steps, requests, _ = attn_out.shape
    width = store_b.shape[2]
    rows = steps * requests
    share = rows // WINDOW
    f32 = jnp.float32
    me = lax.axis_index("tensor").astype(jnp.int32).reshape(1)
    x = attn_out.reshape(rows, depth)

    wish = local_call(
        lambda *refs: wish_kernel(stored, *refs),
        jax.ShapeDtypeStruct((replicas, 8, 128), jnp.int32), 0, 1 << 17,
        (adapter_lists, placement_map),
    )
    asked = lax.all_to_all(wish, "dp", split_axis=0, concat_axis=0, tiled=True)

    x_later, wish = lax.optimization_barrier((x, wish))
    partial = jnp.einsum("icw,ri->crw", base_weight.reshape(depth, columns, width), x_later,
                         preferred_element_type=f32)
    base = lax.psum_scatter(partial, "tensor", scatter_dimension=0, tiled=True)[0]

    hold = local_call(
        lambda *refs: hold_kernel(stored, steps, *refs),
        jax.ShapeDtypeStruct((rows, 128), jnp.int32), 0, 1 << 17,
        (adapter_lists, placement_map, request_slot),
    )

    def fetch(store):
        shape = (replicas,) + store.shape[1:]
        picked = local_call(
            pick_kernel, jax.ShapeDtypeStruct(shape, store.dtype), 0, 5 << 20, (), asked, store
        )
        return lax.all_to_all(picked, "dp", split_axis=0, concat_axis=0, tiled=True)

    got_a = fetch(store_a)
    got_b = fetch(store_b)
    parts = local_call(
        shrink_kernel, (jax.ShapeDtypeStruct((share, rank), f32),) * WINDOW,
        2 * rows * replicas * depth * rank, 3 << 20, (me,), hold, x, got_a,
        scratch=(pltpu.VMEM((rows, rank), f32),),
    )
    shrink = sum_over_tensor(parts)
    out = local_call(
        final_kernel, jax.ShapeDtypeStruct((rows, width), jnp.bfloat16),
        4 * rows * replicas * rank * width, 3 << 20, (me,), hold, *shrink, got_b, base,
        scratch=(pltpu.VMEM((rows, width), f32),),
    )
    return out.reshape(steps, requests, width)


def solution(mesh):
    placed = (
        P(None, "dp", "tensor"),
        P("tensor", None),
        P("dp", "tensor", None),
        P("dp", None, "tensor"),
        P("dp", None),
        P(),
        P("dp"),
    )
    return jax.shard_map(
        on_device, mesh=mesh, in_specs=placed, out_specs=P(None, "dp", "tensor"), check_vma=False
    )
```

```python
import jax
import jax.numpy as jnp
from jax import lax
from jax.experimental import pallas as pl
from jax.experimental.pallas import tpu as pltpu
from jax.sharding import PartitionSpec as P

MIB = 1024 * 1024
SMEM, VMEM, HBM = (pl.BlockSpec(memory_space=m) for m in (pltpu.SMEM, pltpu.VMEM, pltpu.HBM))
DMA = pltpu.SemaphoreType.DMA
MOST_CHUNKS = 8
ALL = 60


def local_call(body, outs, flops, moved, in_specs, out_specs, scratch, operands, grid=(), limit=16):
    return pl.pallas_call(
        body,
        out_shape=outs,
        grid=grid,
        in_specs=in_specs,
        out_specs=out_specs,
        scratch_shapes=scratch,
        compiler_params=pltpu.CompilerParams(vmem_limit_bytes=limit * MIB),
        cost_estimate=pl.CostEstimate(flops=flops, bytes_accessed=moved, transcendentals=0),
    )(*operands)


def wish_kernel(stored, list_ref, place_ref, wish_ref):
    wish_ref[...] = jnp.zeros_like(wish_ref)
    for s in range(list_ref.shape[1]):
        position = place_ref[list_ref[0, s]]
        slot = lax.rem(position, stored)
        wish_ref[lax.div(position, stored)] = jnp.full(wish_ref.shape[1:], slot, jnp.int32)


def base_kernel(x_ref, weight_ref, out_ref):
    x = x_ref[...]
    width = out_ref.shape[2]
    for c in range(out_ref.shape[0]):
        out_ref[c] = jnp.dot(
            x, weight_ref[:, c * width:(c + 1) * width], preferred_element_type=jnp.float32
        )


def pick(asked_ref, store_ref, out_ref, sems):
    def copy(q):
        return pltpu.make_async_copy(
            store_ref.at[asked_ref[q, 0, 0]], out_ref.at[q], sems.at[q]
        )

    count = out_ref.shape[0]
    pl.loop(0, count)(lambda q: copy(q).start())
    return lambda: pl.loop(0, count)(lambda q: copy(q).wait())


def pick_kernel(asked_ref, store_ref, out_ref, sems):
    pick(asked_ref, store_ref, out_ref, sems)()


def pick_hold_kernel(stored, steps, asked_ref, list_ref, place_ref, slot_ref, store_ref,
                     out_ref, hold_ref, sems):
    finish = pick(asked_ref, store_ref, out_ref, sems)
    requests = slot_ref.shape[0]

    @pl.loop(0, requests, unroll=8)
    def _(r):
        holder = lax.div(place_ref[list_ref[0, slot_ref[r]]], stored)
        for step in range(steps):
            hold_ref[pl.ds(step * requests + r, 1), :] = jnp.full((1, 128), holder, jnp.int32)

    finish()


def shrink_kernel(hold_ref, x_ref, panels_ref, out_ref):
    hold = hold_ref[...]
    x = x_ref[...]
    out_ref[...] = jnp.zeros_like(out_ref)

    @pl.loop(0, panels_ref.shape[0], unroll=4)
    def _(q):
        product = jnp.dot(x, panels_ref[q], preferred_element_type=jnp.float32)
        out_ref[...] = jnp.where(hold == q, product, out_ref[...])


def final_kernel(hold_ref, shrink_ref, other_ref, panels_hbm, base_hbm, out_ref,
                 total_ref, panels_ref, base_ref, sems):
    chunks = sems.shape[0] - 1
    each = panels_ref.shape[0] // chunks

    def copy(c):
        part = pl.ds(c * each, each)
        return pltpu.make_async_copy(panels_hbm.at[part], panels_ref.at[part], sems.at[c])

    base_copy = pltpu.make_async_copy(base_hbm, base_ref, sems.at[chunks])
    for c in range(chunks):
        copy(c).start()
    base_copy.start()

    hold = hold_ref[...]
    hold = jnp.concatenate([hold] * (total_ref.shape[1] // hold.shape[1]), axis=1)
    shrink = shrink_ref[...] + other_ref[...]
    high = shrink.astype(jnp.bfloat16)
    low = (shrink - high.astype(jnp.float32)).astype(jnp.bfloat16)
    both = jnp.concatenate([high, low], axis=1)
    total_ref[...] = jnp.zeros_like(total_ref)

    for c in range(chunks):
        copy(c).wait()
        for q in range(c * each, (c + 1) * each):
            panel = panels_ref[q]
            product = jnp.dot(
                both, jnp.concatenate([panel, panel], axis=0), preferred_element_type=jnp.float32
            )
            total_ref[...] = jnp.where(hold == q, product, total_ref[...])

    base_copy.wait()
    out_ref[...] = (base_ref[...] + total_ref[...]).astype(out_ref.dtype)


def across(value, bit, size):
    return lax.ppermute(value, "tensor", [(i, i ^ bit) for i in range(size)])


def on_device(attn_out, base_weight, store_a, store_b, adapter_lists, placement_map, request_slot):
    replicas = lax.axis_size("dp")
    columns = lax.axis_size("tensor")
    stored, depth, rank = store_a.shape
    steps, requests, _ = attn_out.shape
    width = store_b.shape[2]
    rows = steps * requests
    f32, bf16, i32 = jnp.float32, jnp.bfloat16, jnp.int32
    shaped = jax.ShapeDtypeStruct
    x = attn_out.reshape(rows, depth)

    wish = local_call(
        lambda *refs: wish_kernel(stored, *refs), shaped((replicas, 1, 128), i32), 0, 1 << 14,
        [SMEM, SMEM], VMEM, [], (adapter_lists, placement_map),
    )
    asked = lax.all_to_all(wish, "dp", split_axis=0, concat_axis=0, tiled=True)

    partial = local_call(
        base_kernel, shaped((columns, rows, width), f32),
        2 * rows * depth * columns * width, 5 << 20,
        [pl.BlockSpec((rows, depth), lambda i: (0, 0)),
         pl.BlockSpec((depth, 4 * width), lambda i: (0, i))],
        pl.BlockSpec((4, rows, width), lambda i: (i, 0, 0)), [], (x, base_weight),
        grid=(columns // 4,), limit=ALL,
    )
    base = lax.psum_scatter(partial, "tensor", scatter_dimension=0, tiled=True)[0]

    picked_a = local_call(
        pick_kernel, shaped((replicas,) + store_a.shape[1:], bf16), 0, 4 << 20,
        [SMEM, VMEM], HBM, [DMA((replicas,))], (asked, store_a), limit=ALL,
    )
    got_a = lax.all_to_all(picked_a, "dp", split_axis=0, concat_axis=0, tiled=True)
    picked_b, hold = local_call(
        lambda *refs: pick_hold_kernel(stored, steps, *refs),
        (shaped((replicas,) + store_b.shape[1:], bf16), shaped((rows, 128), i32)), 0, 4 << 20,
        [SMEM, SMEM, SMEM, SMEM, VMEM], (HBM, VMEM), [DMA((replicas,))],
        (asked, adapter_lists, placement_map, request_slot, store_b),
    )
    got_b = lax.all_to_all(picked_b, "dp", split_axis=0, concat_axis=0, tiled=True)

    shrink = local_call(
        shrink_kernel, shaped((rows, rank), f32), 2 * rows * replicas * depth * rank, 3 << 20,
        [VMEM] * 3, VMEM, [], (hold, x, got_a),
    )
    bit = columns // 2
    while bit > 1:
        shrink = shrink + across(shrink, bit, columns)
        bit //= 2
    out = local_call(
        final_kernel, shaped((rows, width), bf16),
        4 * rows * replicas * rank * width, 3 << 20,
        [VMEM, VMEM, VMEM, HBM, HBM], VMEM,
        [pltpu.VMEM((rows, width), f32), pltpu.VMEM(got_b.shape, bf16),
         pltpu.VMEM((rows, width), f32), DMA((min(MOST_CHUNKS, replicas) + 1,))],
        (hold, shrink, across(shrink, 1, columns), got_b, base), limit=40,
    )
    return out.reshape(steps, requests, width)


def solution(mesh):
    placed = (
        P(None, "dp", "tensor"),
        P("tensor", None),
        P("dp", "tensor", None),
        P("dp", None, "tensor"),
        P("dp", None),
        P(),
        P("dp"),
    )
    return jax.shard_map(
        on_device, mesh=mesh, in_specs=placed, out_specs=P(None, "dp", "tensor"), check_vma=False
    )
```

```python
import jax
import jax.numpy as jnp
from jax import lax
from jax.experimental import pallas as pl
from jax.experimental.pallas import tpu as pltpu
from jax.sharding import PartitionSpec as P

MIB = 1024 * 1024
SMEM, VMEM, HBM = (pl.BlockSpec(memory_space=m) for m in (pltpu.SMEM, pltpu.VMEM, pltpu.HBM))
DMA = pltpu.SemaphoreType.DMA
MOST_CHUNKS = 8
ADD_LONG = 2 * 10**10
LONG = 2275 * 10**7
ALL = 60


def local_call(body, outs, flops, moved, in_specs, out_specs, scratch, operands, grid=(), limit=16):
    return pl.pallas_call(
        body,
        out_shape=outs,
        grid=grid,
        in_specs=in_specs,
        out_specs=out_specs,
        scratch_shapes=scratch,
        compiler_params=pltpu.CompilerParams(vmem_limit_bytes=limit * MIB),
        cost_estimate=pl.CostEstimate(flops=flops, bytes_accessed=moved, transcendentals=0),
    )(*operands)


def wish_kernel(stored, list_ref, place_ref, wish_ref):
    wish_ref[...] = jnp.zeros_like(wish_ref)
    for s in range(list_ref.shape[1]):
        position = place_ref[list_ref[0, s]]
        slot = lax.rem(position, stored)
        wish_ref[lax.div(position, stored)] = jnp.full(wish_ref.shape[1:], slot, jnp.int32)


def base_kernel(x_ref, weight_ref, out_ref):
    x = x_ref[...]
    width = out_ref.shape[2]
    for c in range(out_ref.shape[0]):
        out_ref[c] = jnp.dot(
            x, weight_ref[:, c * width:(c + 1) * width], preferred_element_type=jnp.float32
        )


def pick(asked_ref, store_ref, out_ref, sems):
    def copy(q):
        return pltpu.make_async_copy(
            store_ref.at[asked_ref[q, 0, 0]], out_ref.at[q], sems.at[q]
        )

    count = out_ref.shape[0]
    pl.loop(0, count)(lambda q: copy(q).start())
    return lambda: pl.loop(0, count)(lambda q: copy(q).wait())


def pick_kernel(asked_ref, store_ref, out_ref, sems):
    pick(asked_ref, store_ref, out_ref, sems)()


def pick_hold_kernel(stored, steps, asked_ref, list_ref, place_ref, slot_ref, store_ref,
                     out_ref, hold_ref, sems):
    finish = pick(asked_ref, store_ref, out_ref, sems)
    requests = slot_ref.shape[0]

    @pl.loop(0, requests, unroll=8)
    def _(r):
        holder = lax.div(place_ref[list_ref[0, slot_ref[r]]], stored)
        for step in range(steps):
            hold_ref[pl.ds(step * requests + r, 1), :] = jnp.full((1, 128), holder, jnp.int32)

    finish()


def shrink_kernel(me_ref, hold_ref, x_ref, panels_ref, mine_ref, other_ref, total_ref):
    hold = hold_ref[...]
    x = x_ref[...]
    total_ref[...] = jnp.zeros_like(total_ref)

    @pl.loop(0, panels_ref.shape[0], unroll=4)
    def _(q):
        product = jnp.dot(x, panels_ref[q], preferred_element_type=jnp.float32)
        total_ref[...] = jnp.where(hold == q, product, total_ref[...])

    mine, other = halves(me_ref, total_ref)
    mine_ref[...] = total_ref[mine, :]
    other_ref[...] = total_ref[other, :]


def add_kernel(a_ref, b_ref, out_ref):
    out_ref[...] = a_ref[...] + b_ref[...]


def halves(me_ref, ref):
    half = ref.shape[0] // 2
    odd = lax.rem(me_ref[0], 2)
    return (pl.ds(pl.multiple_of(odd * half, half), half),
            pl.ds(pl.multiple_of((1 - odd) * half, half), half))


def final_kernel(me_ref, hold_ref, mine_ref, other_ref, panels_hbm, base_hbm, out_ref,
                 shrink_ref, total_ref, panels_ref, base_ref, sems):
    chunks = sems.shape[0] - 1
    each = panels_ref.shape[0] // chunks

    def copy(c):
        part = pl.ds(c * each, each)
        return pltpu.make_async_copy(panels_hbm.at[part], panels_ref.at[part], sems.at[c])

    base_copy = pltpu.make_async_copy(base_hbm, base_ref, sems.at[chunks])
    for c in range(chunks):
        copy(c).start()
    base_copy.start()

    hold = hold_ref[...]
    hold = jnp.concatenate([hold] * (total_ref.shape[1] // hold.shape[1]), axis=1)
    mine, other = halves(me_ref, shrink_ref)
    shrink_ref[mine, :] = mine_ref[...]
    shrink_ref[other, :] = other_ref[...]
    shrink = shrink_ref[...]
    high = shrink.astype(jnp.bfloat16)
    low = (shrink - high.astype(jnp.float32)).astype(jnp.bfloat16)
    both = jnp.concatenate([high, low], axis=1)
    total_ref[...] = jnp.zeros_like(total_ref)

    for c in range(chunks):
        copy(c).wait()
        for q in range(c * each, (c + 1) * each):
            panel = panels_ref[q]
            product = jnp.dot(
                both, jnp.concatenate([panel, panel], axis=0), preferred_element_type=jnp.float32
            )
            total_ref[...] = jnp.where(hold == q, product, total_ref[...])

    base_copy.wait()
    out_ref[...] = (base_ref[...] + total_ref[...]).astype(out_ref.dtype)


def across(value, bit, size):
    return lax.ppermute(value, "tensor", [(i, i ^ bit) for i in range(size)])


def on_device(attn_out, base_weight, store_a, store_b, adapter_lists, placement_map, request_slot):
    replicas = lax.axis_size("dp")
    columns = lax.axis_size("tensor")
    stored, depth, rank = store_a.shape
    steps, requests, _ = attn_out.shape
    width = store_b.shape[2]
    rows = steps * requests
    f32, bf16, i32 = jnp.float32, jnp.bfloat16, jnp.int32
    shaped = jax.ShapeDtypeStruct
    x = attn_out.reshape(rows, depth)

    wish = local_call(
        lambda *refs: wish_kernel(stored, *refs), shaped((replicas, 1, 128), i32), 0, 1 << 14,
        [SMEM, SMEM], VMEM, [], (adapter_lists, placement_map),
    )
    asked = lax.all_to_all(wish, "dp", split_axis=0, concat_axis=0, tiled=True)

    partial = local_call(
        base_kernel, shaped((columns, rows, width), f32),
        2 * rows * depth * columns * width, 5 << 20,
        [pl.BlockSpec((rows, depth), lambda i: (0, 0)),
         pl.BlockSpec((depth, 4 * width), lambda i: (0, i))],
        pl.BlockSpec((4, rows, width), lambda i: (i, 0, 0)), [], (x, base_weight),
        grid=(columns // 4,), limit=ALL,
    )
    base = lax.psum_scatter(partial, "tensor", scatter_dimension=0, tiled=True)[0]

    asked, _ = lax.optimization_barrier((asked, partial))
    picked_a = local_call(
        pick_kernel, shaped((replicas,) + store_a.shape[1:], bf16), 0, 4 << 20,
        [SMEM, VMEM], HBM, [DMA((replicas,))], (asked, store_a), limit=ALL,
    )
    got_a = lax.all_to_all(picked_a, "dp", split_axis=0, concat_axis=0, tiled=True)
    picked_b, hold = local_call(
        lambda *refs: pick_hold_kernel(stored, steps, *refs),
        (shaped((replicas,) + store_b.shape[1:], bf16), shaped((rows, 128), i32)), 0, 4 << 20,
        [SMEM, SMEM, SMEM, SMEM, VMEM], (HBM, VMEM), [DMA((replicas,))],
        (asked, adapter_lists, placement_map, request_slot, store_b),
    )
    me = lax.axis_index("tensor").astype(i32).reshape(1)
    half = shaped((rows // 2, rank), f32)
    mine, other = local_call(
        shrink_kernel, (half, half), LONG, 3 << 20,
        [SMEM] + [VMEM] * 3, (VMEM, VMEM), [pltpu.VMEM((rows, rank), f32)], (me, hold, x, got_a),
    )
    picked_b, other = lax.optimization_barrier((picked_b, other))
    got_b = lax.all_to_all(picked_b, "dp", split_axis=0, concat_axis=0, tiled=True)

    mine = local_call(add_kernel, half, ADD_LONG, 1 << 17, [VMEM, VMEM], VMEM, [],
                      (mine, across(other, 1, columns)))
    bit = columns // 2
    while bit > 1:
        mine = mine + across(mine, bit, columns)
        bit //= 2
    out = local_call(
        final_kernel, shaped((rows, width), bf16), LONG, 3 << 20,
        [SMEM, VMEM, VMEM, VMEM, HBM, HBM], VMEM,
        [pltpu.VMEM((rows, rank), f32), pltpu.VMEM((rows, width), f32),
         pltpu.VMEM(got_b.shape, bf16), pltpu.VMEM((rows, width), f32),
         DMA((min(MOST_CHUNKS, replicas) + 1,))],
        (me, hold, mine, across(mine, 1, columns), got_b, base), limit=40,
    )
    return out.reshape(steps, requests, width)


def solution(mesh):
    placed = (
        P(None, "dp", "tensor"),
        P("tensor", None),
        P("dp", "tensor", None),
        P("dp", None, "tensor"),
        P("dp", None),
        P(),
        P("dp"),
    )
    return jax.shard_map(
        on_device, mesh=mesh, in_specs=placed, out_specs=P(None, "dp", "tensor"), check_vma=False
    )
```

```python
import jax
import jax.numpy as jnp
from jax import lax
from jax.experimental import pallas as pl
from jax.experimental.pallas import tpu as pltpu
from jax.sharding import PartitionSpec as P

MIB = 1024 * 1024
SMEM, VMEM, HBM = (pl.BlockSpec(memory_space=m) for m in (pltpu.SMEM, pltpu.VMEM, pltpu.HBM))
DMA = pltpu.SemaphoreType.DMA
MOST_PARTS = 8
ALL = 60


def local_call(body, outs, flops, moved, in_specs, out_specs, scratch, operands, grid=(), limit=16):
    return pl.pallas_call(
        body,
        out_shape=outs,
        grid=grid,
        in_specs=in_specs,
        out_specs=out_specs,
        scratch_shapes=scratch,
        compiler_params=pltpu.CompilerParams(vmem_limit_bytes=limit * MIB),
        cost_estimate=pl.CostEstimate(flops=flops, bytes_accessed=moved, transcendentals=0),
    )(*operands)


def wish_kernel(stored, list_ref, place_ref, wish_ref):
    wish_ref[...] = jnp.zeros_like(wish_ref)
    for s in range(list_ref.shape[1]):
        position = place_ref[list_ref[0, s]]
        slot = lax.rem(position, stored)
        wish_ref[lax.div(position, stored)] = jnp.full(wish_ref.shape[1:], slot, jnp.int32)


def base_kernel(x_ref, weight_ref, out_ref):
    x = x_ref[...]
    width = out_ref.shape[2]
    for c in range(out_ref.shape[0]):
        out_ref[c] = jnp.dot(
            x, weight_ref[:, c * width:(c + 1) * width], preferred_element_type=jnp.float32
        )


def pick_kernel(stored, steps, asked_ref, list_ref, place_ref, slot_ref, a_ref, b_ref,
                out_ref, hold_ref, sems):
    count = out_ref.shape[0]
    depth, width = a_ref.shape[1], b_ref.shape[2]
    rank = b_ref.shape[1]

    def copies(q):
        n = asked_ref[q, 0, 0]
        yield pltpu.make_async_copy(a_ref.at[n], out_ref.at[q, pl.ds(0, depth)], sems.at[q, 0])
        for c in range(width // 128):
            yield pltpu.make_async_copy(
                b_ref.at[n, :, pl.ds(c * 128, 128)],
                out_ref.at[q, pl.ds(depth + c * rank, rank)], sems.at[q, c + 1],
            )

    @pl.loop(0, count)
    def _(q):
        for copy in copies(q):
            copy.start()

    requests = slot_ref.shape[0]

    @pl.loop(0, requests, unroll=8)
    def _(r):
        holder = lax.div(place_ref[list_ref[0, slot_ref[r]]], stored)
        for step in range(steps):
            hold_ref[pl.ds(step * requests + r, 1), :] = jnp.full((1, 128), holder, jnp.int32)

    @pl.loop(0, count)
    def _(q):
        for copy in copies(q):
            copy.wait()


def by_parts(copies):
    for part in copies:
        for copy in part:
            copy.start()
    return lambda c: [copy.wait() for copy in copies[c]]


def shrink_kernel(hold_ref, x_ref, panels_hbm, out_ref, total_ref, panels_ref, sems):
    each = panels_ref.shape[0] // sems.shape[0]
    depth = panels_ref.shape[1]
    ready = by_parts([
        [pltpu.make_async_copy(panels_hbm.at[pl.ds(c * each, each), pl.ds(0, depth)],
                               panels_ref.at[pl.ds(c * each, each)], sems.at[c])]
        for c in range(sems.shape[0])
    ])
    hold = hold_ref[...]
    x = x_ref[...]
    total_ref[...] = jnp.zeros_like(total_ref)
    for c in range(sems.shape[0]):
        ready(c)
        for q in range(c * each, (c + 1) * each):
            product = jnp.dot(x, panels_ref[q], preferred_element_type=jnp.float32)
            total_ref[...] = jnp.where(hold == q, product, total_ref[...])

    share = out_ref.shape[1]
    for z in range(out_ref.shape[0]):
        if z * share < total_ref.shape[0]:
            out_ref[z] = total_ref[z * share:(z + 1) * share, :]
        else:
            out_ref[z] = jnp.zeros(out_ref.shape[1:], jnp.float32)


def final_kernel(hold_ref, shrink_ref, panels_hbm, base_ref, out_ref, total_ref, panels_ref, sems):
    rows, width = out_ref.shape
    rank = shrink_ref.shape[2]
    depth = panels_hbm.shape[1] - rank * (width // 128)
    each = panels_ref.shape[0] // sems.shape[0]
    ready = by_parts([
        [pltpu.make_async_copy(
            panels_hbm.at[pl.ds(c * each, each), pl.ds(depth + k * rank, rank)],
            panels_ref.at[pl.ds(c * each, each), :, pl.ds(k * 128, 128)], sems.at[c, k])
         for k in range(width // 128)]
        for c in range(sems.shape[0])
    ])
    hold = hold_ref[...]
    hold = jnp.concatenate([hold] * (width // 128), axis=1)
    share = shrink_ref.shape[1]
    shrink = jnp.concatenate([shrink_ref[z] for z in range(rows // share)], axis=0)
    high = shrink.astype(jnp.bfloat16)
    low = (shrink - high.astype(jnp.float32)).astype(jnp.bfloat16)
    both = jnp.concatenate([high, low], axis=1)
    total_ref[...] = jnp.zeros_like(total_ref)
    for c in range(sems.shape[0]):
        ready(c)
        for q in range(c * each, (c + 1) * each):
            panel = panels_ref[q]
            product = jnp.dot(
                both, jnp.concatenate([panel, panel], axis=0), preferred_element_type=jnp.float32
            )
            total_ref[...] = jnp.where(hold == q, product, total_ref[...])

    out_ref[...] = (base_ref[...] + total_ref[...]).astype(out_ref.dtype)


def on_device(attn_out, base_weight, store_a, store_b, adapter_lists, placement_map, request_slot):
    replicas = lax.axis_size("dp")
    columns = lax.axis_size("tensor")
    stored, depth, rank = store_a.shape
    steps, requests, _ = attn_out.shape
    width = store_b.shape[2]
    rows = steps * requests
    f32, bf16, i32 = jnp.float32, jnp.bfloat16, jnp.int32
    shaped = jax.ShapeDtypeStruct
    x = attn_out.reshape(rows, depth)

    wish = local_call(
        lambda *refs: wish_kernel(stored, *refs), shaped((replicas, 1, 128), i32), 0, 1 << 14,
        [SMEM, SMEM], VMEM, [], (adapter_lists, placement_map), limit=ALL,
    )
    asked = lax.all_to_all(wish, "dp", split_axis=0, concat_axis=0, tiled=True)

    partial = local_call(
        base_kernel, shaped((columns, rows, width), f32),
        2 * rows * depth * columns * width, 5 << 20,
        [pl.BlockSpec((rows, depth), lambda i: (0, 0)),
         pl.BlockSpec((depth, 4 * width), lambda i: (0, i))],
        pl.BlockSpec((4, rows, width), lambda i: (i, 0, 0)), [], (x, base_weight),
        grid=(columns // 4,), limit=ALL,
    )
    base = lax.psum_scatter(partial, "tensor", scatter_dimension=0, tiled=True)[0]

    picked, hold = local_call(
        lambda *refs: pick_kernel(stored, steps, *refs),
        (shaped((replicas, depth + rank * (width // 128), 128), bf16), shaped((rows, 128), i32)),
        0, 8 << 20, [SMEM] * 4 + [VMEM] * 2, (HBM, VMEM), [DMA((replicas, 1 + width // 128))],
        (asked, adapter_lists, placement_map, request_slot, store_a, store_b), limit=ALL,
    )
    panels = lax.all_to_all(picked, "dp", split_axis=0, concat_axis=0, tiled=True)

    share = 16
    parts = min(MOST_PARTS, replicas)
    part = local_call(
        shrink_kernel, shaped((columns, share, rank), f32), 2 * rows * replicas * depth * rank,
        3 << 20, [VMEM, VMEM, HBM], VMEM,
        [pltpu.VMEM((rows, rank), f32), pltpu.VMEM((replicas, depth, rank), bf16), DMA((parts,))],
        (hold, x, panels), limit=ALL,
    )
    part = lax.all_to_all(part, "tensor", split_axis=0, concat_axis=0, tiled=True)
    mine = jnp.broadcast_to(jnp.sum(part, axis=0)[None], part.shape)
    shrink = lax.all_to_all(mine, "tensor", split_axis=0, concat_axis=0, tiled=True)
    out = local_call(
        final_kernel, shaped((rows, width), bf16), 4 * rows * replicas * rank * width, 3 << 20,
        [VMEM, VMEM, HBM, VMEM], VMEM,
        [pltpu.VMEM((rows, width), f32), pltpu.VMEM((replicas, rank, width), bf16),
         DMA((parts, width // 128))],
        (hold, shrink, panels, base), limit=ALL,
    )
    return out.reshape(steps, requests, width)


def solution(mesh):
    placed = (
        P(None, "dp", "tensor"),
        P("tensor", None),
        P("dp", "tensor", None),
        P("dp", None, "tensor"),
        P("dp", None),
        P(),
        P("dp"),
    )
    return jax.shard_map(
        on_device, mesh=mesh, in_specs=placed, out_specs=P(None, "dp", "tensor"), check_vma=False
    )
```

```python
import jax
import jax.numpy as jnp
from jax import lax
from jax.experimental import pallas as pl
from jax.experimental.pallas import tpu as pltpu
from jax.sharding import PartitionSpec as P

MIB = 1024 * 1024
SMEM, VMEM, HBM = (pl.BlockSpec(memory_space=m) for m in (pltpu.SMEM, pltpu.VMEM, pltpu.HBM))
DMA = pltpu.SemaphoreType.DMA
HALF_LONG = 10 ** 8
ADD_LONG = 2*10**10
LONG = 2275 * 10**7
ALL = 60


def local_call(body, outs, flops, moved, in_specs, out_specs, scratch, operands, grid=(), limit=16):
    return pl.pallas_call(
        body,
        out_shape=outs,
        grid=grid,
        in_specs=in_specs,
        out_specs=out_specs,
        scratch_shapes=scratch,
        compiler_params=pltpu.CompilerParams(vmem_limit_bytes=limit * MIB),
        cost_estimate=pl.CostEstimate(flops=flops, bytes_accessed=moved, transcendentals=0),
    )(*operands)


def wish_kernel(stored, list_ref, place_ref, wish_ref):
    wish_ref[...] = jnp.zeros_like(wish_ref)
    for s in range(list_ref.shape[1]):
        position = place_ref[list_ref[0, s]]
        slot = lax.rem(position, stored)
        wish_ref[lax.div(position, stored)] = jnp.full(wish_ref.shape[1:], slot, jnp.int32)


def base_kernel(x_ref, weight_ref, out_ref):
    x = x_ref[...]
    width = out_ref.shape[2]
    for c in range(out_ref.shape[0]):
        out_ref[c] = jnp.dot(
            x, weight_ref[:, c * width:(c + 1) * width], preferred_element_type=jnp.float32
        )


def pick(asked_ref, store_ref, out_ref, sems):
    def copy(q):
        return pltpu.make_async_copy(
            store_ref.at[asked_ref[q, 0, 0]], out_ref.at[q], sems.at[q]
        )

    count = out_ref.shape[0]
    pl.loop(0, count)(lambda q: copy(q).start())
    return lambda: pl.loop(0, count)(lambda q: copy(q).wait())


def pick_kernel(asked_ref, store_ref, out_ref, sems):
    pick(asked_ref, store_ref, out_ref, sems)()


def pick_hold_kernel(stored, steps, asked_ref, list_ref, place_ref, slot_ref, store_ref,
                     out_ref, hold_ref, sems):
    finish = pick(asked_ref, store_ref, out_ref, sems)
    requests = slot_ref.shape[0]

    @pl.loop(0, requests, unroll=8)
    def _(r):
        holder = lax.div(place_ref[list_ref[0, slot_ref[r]]], stored)
        for step in range(steps):
            hold_ref[pl.ds(step * requests + r, 1), :] = jnp.full((1, 128), holder, jnp.int32)

    finish()


def shrink_kernel(me_ref, hold_ref, x_ref, panels_ref, mine_ref, other_ref, total_ref):
    hold = hold_ref[...]
    x = x_ref[...]
    total_ref[...] = jnp.zeros_like(total_ref)

    @pl.loop(0, panels_ref.shape[0], unroll=4)
    def _(q):
        product = jnp.dot(x, panels_ref[q], preferred_element_type=jnp.float32)
        total_ref[...] = jnp.where(hold == q, product, total_ref[...])

    mine, other = halves(me_ref, total_ref)
    mine_ref[...] = total_ref[mine, :]
    other_ref[...] = total_ref[other, :]


def add_kernel(a_ref, b_ref, out_ref):
    out_ref[...] = a_ref[...] + b_ref[...]


def halves(me_ref, ref):
    half = ref.shape[0] // 2
    odd = lax.rem(me_ref[0], 2)
    return (pl.ds(pl.multiple_of(odd * half, half), half),
            pl.ds(pl.multiple_of((1 - odd) * half, half), half))


def up(hold_ref, shrink_ref, rows, panels_ref, total_ref):
    hold = hold_ref[rows, :]
    hold = jnp.concatenate([hold] * (total_ref.shape[1] // hold.shape[1]), axis=1)
    shrink = shrink_ref[...]
    high = shrink.astype(jnp.bfloat16)
    low = (shrink - high.astype(jnp.float32)).astype(jnp.bfloat16)
    both = jnp.concatenate([high, low], axis=1)
    total_ref[...] = jnp.zeros_like(total_ref)

    @pl.loop(0, panels_ref.shape[0], unroll=4)
    def _(q):
        panel = panels_ref[q]
        product = jnp.dot(
            both, jnp.concatenate([panel, panel], axis=0), preferred_element_type=jnp.float32
        )
        total_ref[...] = jnp.where(hold == q, product, total_ref[...])


def first_half_kernel(me_ref, hold_ref, shrink_ref, panels_ref, base_ref, out_ref, total_ref):
    mine, other = halves(me_ref, base_ref)
    up(hold_ref, shrink_ref, mine, panels_ref, total_ref)
    out_ref[mine, :] = base_ref[mine, :] + total_ref[...]
    out_ref[other, :] = base_ref[other, :]


def second_half_kernel(me_ref, hold_ref, shrink_ref, panels_ref, sum_ref, out_ref, total_ref):
    mine, other = halves(me_ref, sum_ref)
    up(hold_ref, shrink_ref, other, panels_ref, total_ref)
    out_ref[mine, :] = sum_ref[mine, :].astype(out_ref.dtype)
    out_ref[other, :] = (sum_ref[other, :] + total_ref[...]).astype(out_ref.dtype)


def across(value, bit, size):
    return lax.ppermute(value, "tensor", [(i, i ^ bit) for i in range(size)])


def on_device(attn_out, base_weight, store_a, store_b, adapter_lists, placement_map, request_slot):
    replicas = lax.axis_size("dp")
    columns = lax.axis_size("tensor")
    stored, depth, rank = store_a.shape
    steps, requests, _ = attn_out.shape
    width = store_b.shape[2]
    rows = steps * requests
    f32, bf16, i32 = jnp.float32, jnp.bfloat16, jnp.int32
    shaped = jax.ShapeDtypeStruct
    x = attn_out.reshape(rows, depth)

    wish = local_call(
        lambda *refs: wish_kernel(stored, *refs), shaped((replicas, 1, 128), i32), 0, 1 << 14,
        [SMEM, SMEM], VMEM, [], (adapter_lists, placement_map), limit=ALL,
    )
    asked = lax.all_to_all(wish, "dp", split_axis=0, concat_axis=0, tiled=True)

    partial = local_call(
        base_kernel, shaped((columns, rows, width), f32),
        2 * rows * depth * columns * width, 5 << 20,
        [pl.BlockSpec((rows, depth), lambda i: (0, 0)),
         pl.BlockSpec((depth, 4 * width), lambda i: (0, i))],
        pl.BlockSpec((4, rows, width), lambda i: (i, 0, 0)), [], (x, base_weight),
        grid=(columns // 4,), limit=ALL,
    )
    base = lax.psum_scatter(partial, "tensor", scatter_dimension=0, tiled=True)[0]

    asked, _ = lax.optimization_barrier((asked, partial))
    picked_a = local_call(
        pick_kernel, shaped((replicas,) + store_a.shape[1:], bf16), 0, 4 << 20,
        [SMEM, VMEM], HBM, [DMA((replicas,))], (asked, store_a), limit=ALL,
    )
    got_a = lax.all_to_all(picked_a, "dp", split_axis=0, concat_axis=0, tiled=True)
    picked_b, hold = local_call(
        lambda *refs: pick_hold_kernel(stored, steps, *refs),
        (shaped((replicas,) + store_b.shape[1:], bf16), shaped((rows, 128), i32)), 0, 4 << 20,
        [SMEM, SMEM, SMEM, SMEM, VMEM], (HBM, VMEM), [DMA((replicas,))],
        (asked, adapter_lists, placement_map, request_slot, store_b),
    )
    me = lax.axis_index("tensor").astype(i32).reshape(1)
    half = shaped((rows // 2, rank), f32)
    mine, other = local_call(
        shrink_kernel, (half, half), LONG, 3 << 20,
        [SMEM] + [VMEM] * 3, (VMEM, VMEM), [pltpu.VMEM((rows, rank), f32)], (me, hold, x, got_a),
    )
    picked_b, other = lax.optimization_barrier((picked_b, other))
    got_b = lax.all_to_all(picked_b, "dp", split_axis=0, concat_axis=0, tiled=True)
    mine = local_call(add_kernel, half, ADD_LONG, 1 << 17, [VMEM, VMEM], VMEM, [],
                      (mine, across(other, 1, columns)))
    mine = mine + across(mine, 2, columns)
    mine = mine + across(mine, 4, columns)
    mine = mine + across(mine, 8, columns)
    other = across(mine, 1, columns)
    def ends(kernel, cost, dtype, shrink, so_far):
        return local_call(
            kernel, shaped((rows, width), dtype), cost, 3 << 20, [SMEM] + [VMEM] * 4, VMEM,
            [pltpu.VMEM((rows // 2, width), f32)], (me, hold, shrink, got_b, so_far),
        )

    out = ends(first_half_kernel, HALF_LONG, f32, mine, base)
    out = ends(second_half_kernel, LONG, bf16, other, out)
    return out.reshape(steps, requests, width)


def solution(mesh):
    placed = (
        P(None, "dp", "tensor"),
        P("tensor", None),
        P("dp", "tensor", None),
        P("dp", None, "tensor"),
        P("dp", None),
        P(),
        P("dp"),
    )
    return jax.shard_map(
        on_device, mesh=mesh, in_specs=placed, out_specs=P(None, "dp", "tensor"), check_vma=False
    )
```

```python
import jax
import jax.numpy as jnp
from jax import lax
from jax.experimental import pallas as pl
from jax.experimental.pallas import tpu as pltpu
from jax.sharding import PartitionSpec as P

MIB = 1024 * 1024
SMEM, VMEM, HBM = (pl.BlockSpec(memory_space=m) for m in (pltpu.SMEM, pltpu.VMEM, pltpu.HBM))
DMA = pltpu.SemaphoreType.DMA
HALF_LONG = 10 ** 8
ADD_LONG = 2*10**10
LONG = 2040 * 10**7
PICK = 48
ALL = 60


def local_call(body, outs, flops, moved, in_specs, out_specs, scratch, operands, grid=(), limit=16):
    return pl.pallas_call(
        body,
        out_shape=outs,
        grid=grid,
        in_specs=in_specs,
        out_specs=out_specs,
        scratch_shapes=scratch,
        compiler_params=pltpu.CompilerParams(vmem_limit_bytes=limit * MIB),
        cost_estimate=pl.CostEstimate(flops=flops, bytes_accessed=moved, transcendentals=0),
    )(*operands)


def wish_kernel(stored, list_ref, place_ref, wish_ref):
    wish_ref[...] = jnp.zeros_like(wish_ref)
    for s in range(list_ref.shape[1]):
        position = place_ref[list_ref[0, s]]
        slot = lax.rem(position, stored)
        wish_ref[lax.div(position, stored)] = jnp.full(wish_ref.shape[1:], slot, jnp.int32)


def base_kernel(x_ref, weight_ref, out_ref):
    x = x_ref[...]
    width = out_ref.shape[2]
    for c in range(out_ref.shape[0]):
        out_ref[c] = jnp.dot(
            x, weight_ref[:, c * width:(c + 1) * width], preferred_element_type=jnp.float32
        )


def pick(asked_ref, store_ref, out_ref, sems):
    def copy(q):
        return pltpu.make_async_copy(
            store_ref.at[asked_ref[q, 0, 0]], out_ref.at[q], sems.at[q]
        )

    count = out_ref.shape[0]
    pl.loop(0, count)(lambda q: copy(q).start())
    return lambda: pl.loop(0, count)(lambda q: copy(q).wait())


def pick_kernel(asked_ref, store_ref, out_ref, sems):
    pick(asked_ref, store_ref, out_ref, sems)()


def pick_hold_kernel(stored, steps, asked_ref, list_ref, place_ref, slot_ref, store_ref,
                     out_ref, hold_ref, sems):
    finish = pick(asked_ref, store_ref, out_ref, sems)
    requests = slot_ref.shape[0]

    @pl.loop(0, requests, unroll=8)
    def _(r):
        holder = lax.div(place_ref[list_ref[0, slot_ref[r]]], stored)
        for step in range(steps):
            hold_ref[pl.ds(step * requests + r, 1), :] = jnp.full((1, 128), holder, jnp.int32)

    finish()


def shrink_kernel(me_ref, hold_ref, x_ref, panels_ref, mine_ref, other_ref, total_ref):
    hold = hold_ref[...]
    x = x_ref[...]
    total_ref[...] = jnp.zeros_like(total_ref)

    @pl.loop(0, panels_ref.shape[0], unroll=4)
    def _(q):
        product = jnp.dot(x, panels_ref[q], preferred_element_type=jnp.float32)
        total_ref[...] = jnp.where(hold == q, product, total_ref[...])

    mine, other = halves(me_ref, total_ref)
    mine_ref[...] = total_ref[mine, :]
    other_ref[...] = total_ref[other, :]


def add_kernel(a_ref, b_ref, out_ref):
    out_ref[...] = a_ref[...] + b_ref[...]


def halves(me_ref, ref):
    half = ref.shape[0] // 2
    odd = lax.rem(me_ref[0], 2)
    return (pl.ds(pl.multiple_of(odd * half, half), half),
            pl.ds(pl.multiple_of((1 - odd) * half, half), half))


def up(hold_ref, shrink_ref, rows, panels_ref, total_ref):
    hold = hold_ref[rows, :]
    hold = jnp.concatenate([hold] * (total_ref.shape[1] // hold.shape[1]), axis=1)
    shrink = shrink_ref[...]
    high = shrink.astype(jnp.bfloat16)
    low = (shrink - high.astype(jnp.float32)).astype(jnp.bfloat16)
    both = jnp.concatenate([high, low], axis=1)
    total_ref[...] = jnp.zeros_like(total_ref)

    @pl.loop(0, panels_ref.shape[0], unroll=4)
    def _(q):
        panel = panels_ref[q]
        product = jnp.dot(
            both, jnp.concatenate([panel, panel], axis=0), preferred_element_type=jnp.float32
        )
        total_ref[...] = jnp.where(hold == q, product, total_ref[...])


def first_half_kernel(me_ref, hold_ref, shrink_ref, panels_ref, base_ref, out_ref, total_ref):
    mine, other = halves(me_ref, base_ref)
    up(hold_ref, shrink_ref, mine, panels_ref, total_ref)
    out_ref[mine, :] = base_ref[mine, :] + total_ref[...]
    out_ref[other, :] = base_ref[other, :]


def second_half_kernel(me_ref, hold_ref, shrink_ref, panels_ref, sum_ref, out_ref, total_ref):
    mine, other = halves(me_ref, sum_ref)
    up(hold_ref, shrink_ref, other, panels_ref, total_ref)
    out_ref[mine, :] = sum_ref[mine, :].astype(out_ref.dtype)
    out_ref[other, :] = (sum_ref[other, :] + total_ref[...]).astype(out_ref.dtype)


def across(value, bit, size):
    return lax.ppermute(value, "tensor", [(i, i ^ bit) for i in range(size)])


def shift(value, by, size):
    return lax.ppermute(value, "tensor", [(i, (i + by) % size) for i in range(size)])


def on_device(attn_out, base_weight, store_a, store_b, adapter_lists, placement_map, request_slot):
    replicas = lax.axis_size("dp")
    columns = lax.axis_size("tensor")
    stored, depth, rank = store_a.shape
    steps, requests, _ = attn_out.shape
    width = store_b.shape[2]
    rows = steps * requests
    f32, bf16, i32 = jnp.float32, jnp.bfloat16, jnp.int32
    shaped = jax.ShapeDtypeStruct
    x = attn_out.reshape(rows, depth)

    wish = local_call(
        lambda *refs: wish_kernel(stored, *refs), shaped((replicas, 1, 128), i32), 0, 1 << 14,
        [SMEM, SMEM], VMEM, [], (adapter_lists, placement_map), limit=ALL,
    )
    asked = lax.all_to_all(wish, "dp", split_axis=0, concat_axis=0, tiled=True)

    partial = local_call(
        base_kernel, shaped((columns, rows, width), f32),
        2 * rows * depth * columns * width, 5 << 20,
        [pl.BlockSpec((rows, depth), lambda i: (0, 0)),
         pl.BlockSpec((depth, 4 * width), lambda i: (0, i))],
        pl.BlockSpec((4, rows, width), lambda i: (i, 0, 0)), [], (x, base_weight),
        grid=(columns // 4,), limit=ALL,
    )
    base = lax.psum_scatter(partial, "tensor", scatter_dimension=0, tiled=True)[0]

    asked, _ = lax.optimization_barrier((asked, partial))
    picked_a = local_call(
        pick_kernel, shaped((replicas,) + store_a.shape[1:], bf16), 0, 4 << 20,
        [SMEM, VMEM], HBM, [DMA((replicas,))], (asked, store_a), limit=PICK,
    )
    got_a = lax.all_to_all(picked_a, "dp", split_axis=0, concat_axis=0, tiled=True)
    picked_b, hold = local_call(
        lambda *refs: pick_hold_kernel(stored, steps, *refs),
        (shaped((replicas,) + store_b.shape[1:], bf16), shaped((rows, 128), i32)), 0, 4 << 20,
        [SMEM, SMEM, SMEM, SMEM, VMEM], (HBM, VMEM), [DMA((replicas,))],
        (asked, adapter_lists, placement_map, request_slot, store_b),
    )
    me = lax.axis_index("tensor").astype(i32).reshape(1)
    half = shaped((rows // 2, rank), f32)
    mine, other = local_call(
        shrink_kernel, (half, half), LONG, 3 << 20,
        [SMEM] + [VMEM] * 3, (VMEM, VMEM), [pltpu.VMEM((rows, rank), f32)], (me, hold, x, got_a),
    )
    mine = mine + across(other, 1, columns)
    picked_b, mine = lax.optimization_barrier((picked_b, mine))
    got_b = lax.all_to_all(picked_b, "dp", split_axis=0, concat_axis=0, tiled=True)
    mine = local_call(add_kernel, half, ADD_LONG, 1 << 17, [VMEM, VMEM], VMEM, [],
                      (mine, across(mine, 2, columns)))
    quarter = columns // 4
    pair = mine + shift(mine, quarter, columns)
    mine = (mine + shift(mine, -quarter, columns)) + shift(pair, quarter, columns)
    other = across(mine, 1, columns)
    def ends(kernel, cost, dtype, shrink, so_far):
        return local_call(
            kernel, shaped((rows, width), dtype), cost, 3 << 20, [SMEM] + [VMEM] * 4, VMEM,
            [pltpu.VMEM((rows // 2, width), f32)], (me, hold, shrink, got_b, so_far),
        )

    out = ends(first_half_kernel, HALF_LONG, f32, mine, base)
    out = ends(second_half_kernel, LONG, bf16, other, out)
    return out.reshape(steps, requests, width)


def solution(mesh):
    placed = (
        P(None, "dp", "tensor"),
        P("tensor", None),
        P("dp", "tensor", None),
        P("dp", None, "tensor"),
        P("dp", None),
        P(),
        P("dp"),
    )
    return jax.shard_map(
        on_device, mesh=mesh, in_specs=placed, out_specs=P(None, "dp", "tensor"), check_vma=False
    )
```

```python
import jax
import jax.numpy as jnp
from jax import lax
from jax.experimental import pallas as pl
from jax.experimental.pallas import tpu as pltpu
from jax.sharding import PartitionSpec as P

MIB = 1024 * 1024
SMEM, VMEM, HBM = (pl.BlockSpec(memory_space=m) for m in (pltpu.SMEM, pltpu.VMEM, pltpu.HBM))
DMA = pltpu.SemaphoreType.DMA
HALF_LONG = 10 ** 8
ADD_LONG = 2*10**10
LONG = 2040 * 10**7
PICK = 48
ALL = 60


def local_call(body, outs, flops, moved, in_specs, out_specs, scratch, operands, grid=(), limit=16):
    return pl.pallas_call(
        body,
        out_shape=outs,
        grid=grid,
        in_specs=in_specs,
        out_specs=out_specs,
        scratch_shapes=scratch,
        compiler_params=pltpu.CompilerParams(vmem_limit_bytes=limit * MIB),
        cost_estimate=pl.CostEstimate(flops=flops, bytes_accessed=moved, transcendentals=0),
    )(*operands)


def wish_kernel(stored, list_ref, place_ref, wish_ref):
    wish_ref[...] = jnp.zeros_like(wish_ref)
    for s in range(list_ref.shape[1]):
        position = place_ref[list_ref[0, s]]
        slot = lax.rem(position, stored)
        wish_ref[lax.div(position, stored)] = jnp.full(wish_ref.shape[1:], slot, jnp.int32)


def base_kernel(x_ref, weight_ref, out_ref):
    x = x_ref[...]
    width = out_ref.shape[2]
    for c in range(out_ref.shape[0]):
        out_ref[c] = jnp.dot(
            x, weight_ref[:, c * width:(c + 1) * width], preferred_element_type=jnp.float32
        )


def pick(asked_ref, store_ref, out_ref, sems):
    def copy(q):
        return pltpu.make_async_copy(
            store_ref.at[asked_ref[q, 0, 0]], out_ref.at[q], sems.at[q]
        )

    count = out_ref.shape[0]
    pl.loop(0, count)(lambda q: copy(q).start())
    return lambda: pl.loop(0, count)(lambda q: copy(q).wait())


def pick_kernel(asked_ref, store_ref, out_ref, sems):
    pick(asked_ref, store_ref, out_ref, sems)()


def pick_hold_kernel(stored, steps, asked_ref, list_ref, place_ref, slot_ref, store_ref,
                     out_ref, hold_ref, sems):
    finish = pick(asked_ref, store_ref, out_ref, sems)
    requests = slot_ref.shape[0]

    @pl.loop(0, requests, unroll=8)
    def _(r):
        holder = lax.div(place_ref[list_ref[0, slot_ref[r]]], stored)
        for step in range(steps):
            hold_ref[pl.ds(step * requests + r, 1), :] = jnp.full((1, 128), holder, jnp.int32)

    finish()


def shrink_kernel(me_ref, hold_ref, x_ref, panels_ref, mine_ref, other_ref, total_ref):
    hold = hold_ref[...]
    x = x_ref[...]
    total_ref[...] = jnp.zeros_like(total_ref)

    @pl.loop(0, panels_ref.shape[0], unroll=16)
    def _(q):
        product = jnp.dot(x, panels_ref[q], preferred_element_type=jnp.float32)
        total_ref[...] = jnp.where(hold == q, product, total_ref[...])

    mine, other = halves(me_ref, total_ref)
    mine_ref[...] = total_ref[mine, :]
    other_ref[...] = total_ref[other, :]


def add_kernel(a_ref, b_ref, out_ref):
    out_ref[...] = a_ref[...] + b_ref[...]


def halves(me_ref, ref):
    half = ref.shape[0] // 2
    odd = lax.rem(me_ref[0], 2)
    return (pl.ds(pl.multiple_of(odd * half, half), half),
            pl.ds(pl.multiple_of((1 - odd) * half, half), half))


def up(hold_ref, shrink_ref, rows, panels_ref, total_ref):
    hold = hold_ref[rows, :]
    hold = jnp.concatenate([hold] * (total_ref.shape[1] // hold.shape[1]), axis=1)
    shrink = shrink_ref[...]
    high = shrink.astype(jnp.bfloat16)
    low = (shrink - high.astype(jnp.float32)).astype(jnp.bfloat16)
    both = jnp.concatenate([high, low], axis=1)
    total_ref[...] = jnp.zeros_like(total_ref)

    @pl.loop(0, panels_ref.shape[0], unroll=16)
    def _(q):
        panel = panels_ref[q]
        product = jnp.dot(
            both, jnp.concatenate([panel, panel], axis=0), preferred_element_type=jnp.float32
        )
        total_ref[...] = jnp.where(hold == q, product, total_ref[...])


def first_half_kernel(me_ref, hold_ref, shrink_ref, panels_ref, base_ref, out_ref, total_ref):
    mine, other = halves(me_ref, base_ref)
    up(hold_ref, shrink_ref, mine, panels_ref, total_ref)
    out_ref[mine, :] = base_ref[mine, :] + total_ref[...]
    out_ref[other, :] = base_ref[other, :]


def second_half_kernel(me_ref, hold_ref, shrink_ref, panels_ref, sum_ref, out_ref, total_ref):
    mine, other = halves(me_ref, sum_ref)
    up(hold_ref, shrink_ref, other, panels_ref, total_ref)
    out_ref[mine, :] = sum_ref[mine, :].astype(out_ref.dtype)
    out_ref[other, :] = (sum_ref[other, :] + total_ref[...]).astype(out_ref.dtype)


def across(value, bit, size):
    return lax.ppermute(value, "tensor", [(i, i ^ bit) for i in range(size)])


def shift(value, by, size):
    return lax.ppermute(value, "tensor", [(i, (i + by) % size) for i in range(size)])


def on_device(attn_out, base_weight, store_a, store_b, adapter_lists, placement_map, request_slot):
    replicas = lax.axis_size("dp")
    columns = lax.axis_size("tensor")
    stored, depth, rank = store_a.shape
    steps, requests, _ = attn_out.shape
    width = store_b.shape[2]
    rows = steps * requests
    f32, bf16, i32 = jnp.float32, jnp.bfloat16, jnp.int32
    shaped = jax.ShapeDtypeStruct
    x = attn_out.reshape(rows, depth)

    wish = local_call(
        lambda *refs: wish_kernel(stored, *refs), shaped((replicas, 1, 128), i32), 0, 1 << 14,
        [SMEM, SMEM], VMEM, [], (adapter_lists, placement_map), limit=ALL,
    )
    asked = lax.all_to_all(wish, "dp", split_axis=0, concat_axis=0, tiled=True)

    partial = local_call(
        base_kernel, shaped((columns, rows, width), f32),
        2 * rows * depth * columns * width, 5 << 20,
        [pl.BlockSpec((rows, depth), lambda i: (0, 0)),
         pl.BlockSpec((depth, 4 * width), lambda i: (0, i))],
        pl.BlockSpec((4, rows, width), lambda i: (i, 0, 0)), [], (x, base_weight),
        grid=(columns // 4,), limit=ALL,
    )
    base = lax.psum_scatter(partial, "tensor", scatter_dimension=0, tiled=True)[0]

    asked, _ = lax.optimization_barrier((asked, partial))
    picked_a = local_call(
        pick_kernel, shaped((replicas,) + store_a.shape[1:], bf16), 0, 4 << 20,
        [SMEM, VMEM], HBM, [DMA((replicas,))], (asked, store_a), limit=PICK,
    )
    got_a = lax.all_to_all(picked_a, "dp", split_axis=0, concat_axis=0, tiled=True)
    picked_b, hold = local_call(
        lambda *refs: pick_hold_kernel(stored, steps, *refs),
        (shaped((replicas,) + store_b.shape[1:], bf16), shaped((rows, 128), i32)), 0, 4 << 20,
        [SMEM, SMEM, SMEM, SMEM, VMEM], (HBM, VMEM), [DMA((replicas,))],
        (asked, adapter_lists, placement_map, request_slot, store_b),
    )
    me = lax.axis_index("tensor").astype(i32).reshape(1)
    half = shaped((rows // 2, rank), f32)
    mine, other = local_call(
        shrink_kernel, (half, half), LONG, 3 << 20,
        [SMEM] + [VMEM] * 3, (VMEM, VMEM), [pltpu.VMEM((rows, rank), f32)], (me, hold, x, got_a),
    )
    mine = mine + across(other, 1, columns)
    picked_b, mine = lax.optimization_barrier((picked_b, mine))
    got_b = lax.all_to_all(picked_b, "dp", split_axis=0, concat_axis=0, tiled=True)
    mine = local_call(add_kernel, half, ADD_LONG, 1 << 17, [VMEM, VMEM], VMEM, [],
                      (mine, across(mine, 2, columns)))
    quarter = columns // 4
    pair = mine + shift(mine, quarter, columns)
    mine = (mine + shift(mine, -quarter, columns)) + shift(pair, quarter, columns)
    other = across(mine, 1, columns)
    def ends(kernel, cost, dtype, shrink, so_far):
        return local_call(
            kernel, shaped((rows, width), dtype), cost, 3 << 20, [SMEM] + [VMEM] * 4, VMEM,
            [pltpu.VMEM((rows // 2, width), f32)], (me, hold, shrink, got_b, so_far),
        )

    out = ends(first_half_kernel, HALF_LONG, f32, mine, base)
    out = ends(second_half_kernel, LONG, bf16, other, out)
    return out.reshape(steps, requests, width)


def solution(mesh):
    placed = (
        P(None, "dp", "tensor"),
        P("tensor", None),
        P("dp", "tensor", None),
        P("dp", None, "tensor"),
        P("dp", None),
        P(),
        P("dp"),
    )
    return jax.shard_map(
        on_device, mesh=mesh, in_specs=placed, out_specs=P(None, "dp", "tensor"), check_vma=False
    )
```
